128 devices in a mesh: batch: 128 (over x, y, z, core).
Axes of the slice: x: 4, y: 4, z: 4, core: 2. Of those that a mesh axis runs over, the one named last changes fastest.
Arguments:
- images: bfloat16 [65536, 1152], P('batch'), may hold values from -6 to 6
- texts: bfloat16 [65536, 1152], P('batch'), may hold values from -6 to 6
Outputs:
- row_loss: float32 [65536], P('batch')
- grad_images: float32 [65536, 1152], P('batch')
- grad_texts: float32 [65536, 1152], P('batch')
The draws below stay inside these ranges and needn't reach their ends.
All inputs are finite; a program needn't handle non-finite values.
Results may differ from the reference program's by a relative error of at most 0.0018.
Values may be sent and summed in bfloat16 or wider, within the bound.
A program may use at most 128 MiB of HBM per device.

```python
import math
import jax
import jax.numpy as jnp
from jax import lax

D = 1152
ROWS = 512
SECTIONS = 3
GROUPS = 16
GROUP_ROWS = 4096
TOKENS = 65536


def steps_of(key, shape, pieces, low, largest):
    def one(position, parts):
        draws = jax.random.uniform(jax.random.fold_in(jax.random.fold_in(key, 6), position), (parts,), jnp.float32, low / len(pieces), largest / len(pieces))
        return jnp.repeat(jnp.exp(draws), shape[position] // parts).reshape((-1,) + (1,) * (len(shape) - position - 1))

    level = one(*pieces[0])
    for cut in pieces[1:]:
        level = level * one(*cut)
    return level


def gaussian(key, dims, spread, most, cuts=(), kind=jnp.bfloat16):
    entries = spread * jax.random.normal(key, dims, jnp.float32)
    if cuts:
        entries = entries * steps_of(key, dims, cuts, -0.22, 0.18)
    return jnp.clip(entries, -most, most).astype(kind)


def setup_inputs(seed: int = 0) -> dict:
    seeds = jax.random.split(jax.random.key(seed), 3)
    images = gaussian(seeds[0], (TOKENS, D), 1.0, 6.0, ((0, 128),))
    texts = gaussian(seeds[1], (TOKENS, D), 1.0, 6.0, ((0, 128),))
    return {"images": images, "texts": texts}


def group_terms(pair):
    group_images, group_texts = pair
    scale = 2.0 / math.sqrt(D)
    logits = jnp.dot(group_images, group_texts.T, preferred_element_type=jnp.float32) * scale - 1.0
    match = jnp.eye(GROUP_ROWS, dtype=bool)
    signed = jnp.where(match, logits, -logits)
    row_loss = lax.optimization_barrier(jnp.mean(-jax.nn.log_sigmoid(signed), axis=1))
    coef = (scale * (jax.nn.sigmoid(logits) - match.astype(jnp.float32))).astype(jnp.bfloat16)
    grad_images = jnp.dot(coef, group_texts, preferred_element_type=jnp.float32)
    grad_texts = jnp.dot(coef.T, group_images, preferred_element_type=jnp.float32)
    return (row_loss, grad_images, grad_texts)

def regroup(array):
    members = 2 ** SECTIONS
    strided = array.reshape((members, GROUPS, ROWS) + array.shape[1:])
    strided = jnp.swapaxes(strided, 0, 1)
    return strided.reshape((GROUPS, GROUP_ROWS) + array.shape[1:])

def ungroup(array):
    members = 2 ** SECTIONS
    strided = array.reshape((GROUPS, members, ROWS) + array.shape[2:])
    strided = jnp.swapaxes(strided, 0, 1)
    return strided.reshape((TOKENS,) + array.shape[2:])

def reference(images, texts):
    row_loss, grad_images, grad_texts = lax.map(group_terms, (regroup(images), regroup(texts)))
    return (ungroup(row_loss), ungroup(grad_images), ungroup(grad_texts))
```

```python
import functools
import math

import jax
import jax.numpy as jnp
from jax import lax
from jax.experimental import pallas as pl
from jax.experimental.pallas import tpu as pltpu
from jax.sharding import PartitionSpec as P

MESH = pl.DeviceIdType.MESH
F32 = jnp.float32
BF16 = jnp.bfloat16
OWN, YP, AP, FAR = 0, 1, 2, 3
CHUNK = 128
HALF = 256


def pair_terms(products, scale, match):
    logits = products * scale - 1.0
    small = jnp.exp(-jnp.abs(logits))
    inverse = 1.0 / (1.0 + small)
    sig = jnp.where(logits >= 0.0, inverse, small * inverse)
    tail = jnp.where(
        small < 1e-2,
        small * (1.0 - small * (0.5 - small * (1.0 / 3.0))),
        jnp.log(1.0 + small),
    )
    if match is None:
        return (scale * sig).astype(BF16), jnp.maximum(logits, 0.0) + tail
    coef = (scale * (sig - match.astype(F32))).astype(BF16)
    return coef, jnp.maximum(jnp.where(match, -logits, logits), 0.0) + tail


def kernel(
    images, texts, row_loss, grad_images, grad_texts,
    im, tx, coef, losses, far_losses, grad_b, hold,
    out_y, out_a, out_far, out_b, in_y, in_a, in_far, in_b,
    send, recv, local,
):
    rows, width = images.shape
    scale = 2.0 / math.sqrt(width)
    me = lax.axis_index("batch")
    core = lax.rem(me, 2)
    x = lax.div(me, 32)
    near = me + 32 * (1 - 2 * lax.rem(x, 2))
    other = me + 32 * (3 - 2 * x)
    a = near * (1 - core) + other * core
    b = other * (1 - core) + near * core
    y = me + 16 * (1 - 2 * lax.rem(lax.div(me, 16), 2))

    count = [0]

    def to(src, dst, device):
        k = count[0]
        count[0] += 1
        return pltpu.make_async_remote_copy(
            src, dst, send.at[k], recv.at[k], device_id=(device,), device_id_type=MESH
        )

    chunks = [pl.ds(k * CHUNK, CHUNK) for k in range(rows // CHUNK)]
    image_b = [to(images.at[c], im.at[pl.ds(rows + c.start, CHUNK)], b) for c in chunks]
    text_y = [to(texts.at[c], tx.at[YP, c], y) for c in chunks]
    text_a = [to(texts.at[c], tx.at[AP, c], a) for c in chunks]
    text_far = [
        to(tx.at[AP, c], tx.at[FAR, c], y) if c.start < CHUNK else to(tx.at[YP, c], tx.at[FAR, c], a)
        for c in chunks
    ]
    back_far = [
        to(out_far.at[c], in_far.at[c], y if c.start < CHUNK else a) for c in chunks
    ]
    back_y = [to(out_y.at[c], in_y.at[c], y) for c in chunks]
    back_a = [to(out_a.at[c], in_a.at[c], a) for c in chunks]
    back_b = [to(out_b.at[c], in_b.at[c], b) for c in chunks]
    back_loss = to(losses.at[1], far_losses, b)

    barrier = pltpu.get_barrier_semaphore()
    for device in (a, b, y):
        pl.semaphore_signal(barrier, inc=1, device_id=(device,), device_id_type=MESH)
    pl.semaphore_wait(barrier, 3)

    for copy in image_b + text_y:
        copy.start()
    own_text = pltpu.make_async_copy(texts, tx.at[OWN], local.at[0])
    own_image = pltpu.make_async_copy(images, im.at[pl.ds(0, rows)], local.at[1])
    own_text.start()
    own_image.start()
    own_text.wait()
    own_image.wait()

    def pairs(slot, first, size, side, diagonal):
        columns = pl.ds(side * rows, rows)
        products = lax.dot_general(
            tx[slot, first:first + size], im[columns], (((1,), (1,)), ((), ())),
            preferred_element_type=F32,
        )
        match = None
        if diagonal:
            match = lax.broadcasted_iota(jnp.int32, (size, rows), 0) == (
                lax.broadcasted_iota(jnp.int32, (size, rows), 1)
            )
        c, loss = pair_terms(products, scale, match)
        coef[:size, columns] = c
        part = loss.reshape(size // 8, 8, rows).sum(0)
        losses[side] = part if slot == OWN else losses[side] + part

    def text_part(size):
        return jnp.dot(coef[:size], im[...], preferred_element_type=F32)

    def image_part(slot, first, size, side):
        return lax.dot_general(
            coef[:size, side * rows:(side + 1) * rows], tx[slot, first:first + size],
            (((0,), (0,)), ((), ())), preferred_element_type=F32,
        )

    def step(slot, first, size):
        for side in (0, 1):
            pairs(slot, first, size, side, False)

    pairs(OWN, 0, rows, 0, True)
    for copy in image_b:
        copy.wait()
    for copy in text_a:
        copy.start()
    pairs(OWN, 0, rows, 1, False)
    grad_texts[...] = text_part(rows)
    grad_images[...] = image_part(OWN, 0, rows, 0)
    grad_b[...] = image_part(OWN, 0, rows, 1)

    for k in (0, 1):
        text_y[k].wait()
    text_far[1].start()
    step(YP, 0, HALF)
    part = text_part(HALF)
    out_y[:CHUNK] = part[:CHUNK].astype(BF16)
    hold[CHUNK:HALF] = part[CHUNK:]
    grad_images[...] += image_part(YP, 0, HALF, 0)
    grad_b[...] += image_part(YP, 0, HALF, 1)

    for k in (0, 1):
        text_a[k].wait()
    text_far[0].start()
    step(AP, 0, HALF)
    part = text_part(HALF)
    hold[:CHUNK] = part[:CHUNK]
    out_a[CHUNK:HALF] = part[CHUNK:].astype(BF16)
    grad_images[...] += image_part(AP, 0, HALF, 0)
    grad_b[...] += image_part(AP, 0, HALF, 1)

    for k in (2, 3):
        text_y[k].wait()
        text_far[k].start()
    step(YP, HALF, HALF)
    hold[HALF:] = text_part(HALF)
    grad_images[...] += image_part(YP, HALF, HALF, 0)
    grad_b[...] += image_part(YP, HALF, HALF, 1)

    for k in (2, 3):
        text_a[k].wait()
    step(AP, HALF, HALF)
    out_a[HALF:] = text_part(HALF).astype(BF16)
    grad_images[...] += image_part(AP, HALF, HALF, 0)
    grad_b[...] += image_part(AP, HALF, HALF, 1)
    back_y[0].start()
    for k in (1, 2, 3):
        back_a[k].start()

    for k in (0, 1):
        text_far[k].wait()
    step(FAR, 0, HALF)
    out_far[:HALF] = text_part(HALF).astype(BF16)
    for k in (0, 1):
        back_far[k].start()
    grad_images[...] += image_part(FAR, 0, HALF, 0)
    grad_b[...] += image_part(FAR, 0, HALF, 1)

    for k in (2, 3):
        text_far[k].wait()
    step(FAR, HALF, HALF)
    back_loss.start()
    out_far[HALF:] = text_part(HALF).astype(BF16)
    for k in (2, 3):
        back_far[k].start()
    out_b[...] = (grad_b[...] + image_part(FAR, HALF, HALF, 1)).astype(BF16)
    for copy in back_b:
        copy.start()
    grad_images[...] += image_part(FAR, HALF, HALF, 0)

    for k, c in enumerate(chunks):
        back_far[k].wait()
        out = out_a if k == 0 else out_y
        out[c] = (hold[c] + in_far[c].astype(F32)).astype(BF16)
        (back_a if k == 0 else back_y)[k].start()
    back_loss.wait()
    row_loss[...] = jnp.sum(losses[0] + far_losses[...], axis=0, keepdims=True) * (1.0 / (8 * rows))
    for k, c in enumerate(chunks):
        back_a[k].wait()
        back_y[k].wait()
        grad_texts[c] += in_a[c].astype(F32) + in_y[c].astype(F32)
    for k, c in enumerate(chunks):
        back_b[k].wait()
        grad_images[c] += in_b[c].astype(F32)


def per_device(images, texts):
    rows, width = images.shape
    block = (rows, width)
    copies = 8 * (rows // CHUNK) + 1
    loss, grad_images, grad_texts = pl.pallas_call(
        kernel,
        out_shape=(
            jax.ShapeDtypeStruct((1, rows), F32),
            jax.ShapeDtypeStruct(block, F32),
            jax.ShapeDtypeStruct(block, F32),
        ),
        in_specs=[pl.BlockSpec(memory_space=pl.ANY)] * 2,
        out_specs=(pl.BlockSpec(memory_space=pltpu.VMEM),) * 3,
        scratch_shapes=[
            pltpu.VMEM((2 * rows, width), BF16),
            pltpu.VMEM((4, rows, width), BF16),
            pltpu.VMEM((rows, 2 * rows), BF16),
            pltpu.VMEM((2, 8, rows), F32),
            pltpu.VMEM((8, rows), F32),
            pltpu.VMEM(block, F32),
            pltpu.VMEM(block, F32),
        ]
        + [pltpu.VMEM(block, BF16)] * 8
        + [
            pltpu.SemaphoreType.DMA((copies,)),
            pltpu.SemaphoreType.DMA((copies,)),
            pltpu.SemaphoreType.DMA((2,)),
        ],
        compiler_params=pltpu.CompilerParams(
            collective_id=0, has_side_effects=True, vmem_limit_bytes=56 * 2**20
        ),
        cost_estimate=pl.CostEstimate(
            flops=6 * 8 * rows * rows * width, bytes_accessed=12 * rows * width,
            transcendentals=3 * 8 * rows * rows,
        ),
    )(images, texts)
    return loss.reshape(rows), grad_images, grad_texts


def solution(mesh):
    placed = (P("batch", None), P("batch", None))
    return jax.shard_map(
        per_device,
        mesh=mesh,
        in_specs=placed,
        out_specs=(P("batch"), P("batch", None), P("batch", None)),
        check_vma=False,
    )
```

```python
import functools
import math

import jax
import jax.numpy as jnp
from jax import lax
from jax.experimental import pallas as pl
from jax.experimental.pallas import tpu as pltpu
from jax.sharding import PartitionSpec as P

MESH = pl.DeviceIdType.MESH
F32 = jnp.float32
BF16 = jnp.bfloat16
OWN, YP, AP, FAR = 0, 1, 2, 3
CHUNK = 128
HALF = 256


def pair_terms(products, scale, match):
    logits = products * scale - 1.0
    small = jnp.exp(-jnp.abs(logits))
    inverse = 1.0 / (1.0 + small)
    sig = jnp.where(logits >= 0.0, inverse, small * inverse)
    tail = jnp.where(
        small < 1e-2,
        small * (1.0 - small * (0.5 - small * (1.0 / 3.0))),
        jnp.log(1.0 + small),
    )
    if match is None:
        return (scale * sig).astype(BF16), jnp.maximum(logits, 0.0) + tail
    coef = (scale * (sig - match.astype(F32))).astype(BF16)
    return coef, jnp.maximum(jnp.where(match, -logits, logits), 0.0) + tail


def kernel(
    images, texts, row_loss, grad_images, grad_texts,
    im, tx, coef, losses, far_losses, grad_b, hold,
    out_y, out_a, out_far, out_b, in_y, in_a, in_far, in_b,
    send, recv, local,
):
    rows, width = images.shape
    scale = 2.0 / math.sqrt(width)
    me = lax.axis_index("batch")
    core = lax.rem(me, 2)
    x = lax.div(me, 32)
    near = me + 32 * (1 - 2 * lax.rem(x, 2))
    other = me + 32 * (3 - 2 * x)
    a = near * (1 - core) + other * core
    b = other * (1 - core) + near * core
    y = me + 16 * (1 - 2 * lax.rem(lax.div(me, 16), 2))

    count = [0]

    def to(src, dst, device):
        k = count[0]
        count[0] += 1
        return pltpu.make_async_remote_copy(
            src, dst, send.at[k], recv.at[k], device_id=(device,), device_id_type=MESH
        )

    chunks = [pl.ds(k * CHUNK, CHUNK) for k in range(rows // CHUNK)]
    image_b = [to(images.at[c], im.at[pl.ds(rows + c.start, CHUNK)], b) for c in chunks]
    text_y = [to(texts.at[c], tx.at[YP, c], y) for c in chunks]
    text_a = [to(texts.at[c], tx.at[AP, c], a) for c in chunks]
    text_far = [
        to(tx.at[AP, c], tx.at[FAR, c], y) if c.start < CHUNK else to(tx.at[YP, c], tx.at[FAR, c], a)
        for c in chunks
    ]
    back_far = [
        to(out_far.at[c], in_far.at[c], y if c.start < CHUNK else a) for c in chunks
    ]
    back_y = [to(out_y.at[c], in_y.at[c], y) for c in chunks]
    back_a = [to(out_a.at[c], in_a.at[c], a) for c in chunks]
    back_b = [to(out_b.at[c], in_b.at[c], b) for c in chunks]
    back_loss = to(losses.at[1], far_losses, b)

    barrier = pltpu.get_barrier_semaphore()
    for device in (a, b, y):
        pl.semaphore_signal(barrier, inc=1, device_id=(device,), device_id_type=MESH)
    pl.semaphore_wait(barrier, 3)

    started = []

    def start(*copies):
        for copy in copies:
            copy.start()
            started.append(copy)

    def arrived(*copies):
        for copy in copies:
            copy.wait_recv()

    start(*image_b, *text_y)
    own_text = pltpu.make_async_copy(texts, tx.at[OWN], local.at[0])
    own_image = pltpu.make_async_copy(images, im.at[pl.ds(0, rows)], local.at[1])
    own_text.start()
    own_image.start()
    own_text.wait()
    own_image.wait()

    def pairs(slot, first, size, side, diagonal=False):
        columns = pl.ds(side * rows, rows)
        products = lax.dot_general(
            tx[slot, first:first + size], im[columns], (((1,), (1,)), ((), ())),
            preferred_element_type=F32,
        )
        match = None
        if diagonal:
            match = lax.broadcasted_iota(jnp.int32, (size, rows), 0) == (
                lax.broadcasted_iota(jnp.int32, (size, rows), 1)
            )
        c, loss = pair_terms(products, scale, match)
        coef[:size, columns] = c
        part = loss.reshape(size // 8, 8, rows).sum(0)
        losses[side] = part if slot == OWN else losses[side] + part

    def text_part(size):
        return jnp.dot(coef[:size], im[...], preferred_element_type=F32)

    def image_part(slot, first, size, side):
        return lax.dot_general(
            coef[:size, side * rows:(side + 1) * rows], tx[slot, first:first + size],
            (((0,), (0,)), ((), ())), preferred_element_type=F32,
        )

    def both_pairs(slot, first):
        pairs(slot, first, HALF, 0)
        pairs(slot, first, HALF, 1)

    def both_images(slot, first):
        grad_images[...] += image_part(slot, first, HALF, 0)
        grad_b[...] += image_part(slot, first, HALF, 1)

    pairs(OWN, 0, rows, 0, True)
    image_b[2].wait_send()
    start(text_a[0])
    image_b[3].wait_send()
    start(*text_a[1:])
    arrived(*image_b)
    pairs(OWN, 0, rows, 1)
    grad_texts[...] = text_part(rows)
    grad_images[...] = image_part(OWN, 0, rows, 0)
    grad_b[...] = image_part(OWN, 0, rows, 1)

    arrived(text_y[0], text_y[1])
    both_pairs(YP, 0)
    part = text_part(HALF)
    out_y[:CHUNK] = part[:CHUNK].astype(BF16)
    hold[CHUNK:HALF] = part[CHUNK:]
    start(text_far[1])
    both_images(YP, 0)

    arrived(text_a[0], text_a[1])
    both_pairs(AP, 0)
    part = text_part(HALF)
    hold[:CHUNK] = part[:CHUNK]
    out_a[CHUNK:HALF] = part[CHUNK:].astype(BF16)
    both_images(AP, 0)

    arrived(text_y[2])
    start(text_far[2], text_far[0])
    arrived(text_y[3])
    start(text_far[3])
    both_pairs(YP, HALF)
    hold[HALF:] = text_part(HALF)
    both_images(YP, HALF)

    arrived(text_a[2], text_a[3])
    both_pairs(AP, HALF)
    out_a[HALF:] = text_part(HALF).astype(BF16)
    start(back_y[0])
    both_images(AP, HALF)

    arrived(text_far[0], text_far[1])
    both_pairs(FAR, 0)
    out_far[:HALF] = text_part(HALF).astype(BF16)
    start(back_far[1], back_far[0])
    both_images(FAR, 0)
    arrived(text_far[2], text_far[3])
    start(back_a[1], back_a[2])
    both_pairs(FAR, HALF)
    start(back_loss)
    out_far[HALF:] = text_part(HALF).astype(BF16)
    start(back_far[2], back_far[3])
    out_b[...] = (grad_b[...] + image_part(FAR, HALF, HALF, 1)).astype(BF16)
    grad_images[...] += image_part(FAR, HALF, HALF, 0)

    def pass_on(k):
        out, back = (out_a, back_a) if k == 0 else (out_y, back_y)
        c = chunks[k]
        arrived(back_far[k])
        out[c] = (hold[c] + in_far[c].astype(F32)).astype(BF16)
        start(back[k])

    pass_on(1)
    start(back_a[3], back_b[0])
    pass_on(2)
    start(*back_b[1:])
    pass_on(3)
    pass_on(0)
    arrived(back_loss)
    row_loss[...] = jnp.sum(losses[0] + far_losses[...], axis=0, keepdims=True) * (1.0 / (8 * rows))
    for k in (1, 2, 3, 0):
        c = chunks[k]
        arrived(back_a[k], back_y[k])
        grad_texts[c] += in_a[c].astype(F32) + in_y[c].astype(F32)
    for k, c in enumerate(chunks):
        arrived(back_b[k])
        grad_images[c] += in_b[c].astype(F32)
    for copy in started:
        if copy is not image_b[2] and copy is not image_b[3]:
            copy.wait_send()


def write_out(*refs):
    sources, targets, done = refs[:3], refs[3:6], refs[6]
    copies = [pltpu.make_async_copy(s, t, done.at[k]) for k, (s, t) in enumerate(zip(sources, targets))]
    for copy in copies:
        copy.start()
    for copy in copies:
        copy.wait()


def per_device(images, texts):
    images = pltpu.with_memory_space_constraint(images, pltpu.HBM)
    texts = pltpu.with_memory_space_constraint(texts, pltpu.HBM)
    rows, width = images.shape
    block = (rows, width)
    copies = 8 * (rows // CHUNK) + 1
    results = pl.pallas_call(
        kernel,
        out_shape=(
            pltpu.VMEM((1, rows), F32),
            pltpu.VMEM(block, F32),
            pltpu.VMEM(block, F32),
        ),
        in_specs=[pl.BlockSpec(memory_space=pl.ANY)] * 2,
        out_specs=(pl.BlockSpec(memory_space=pltpu.VMEM),) * 3,
        scratch_shapes=[
            pltpu.VMEM((2 * rows, width), BF16),
            pltpu.VMEM((4, rows, width), BF16),
            pltpu.VMEM((rows, 2 * rows), BF16),
            pltpu.VMEM((2, 8, rows), F32),
            pltpu.VMEM((8, rows), F32),
            pltpu.VMEM(block, F32),
            pltpu.VMEM(block, F32),
        ]
        + [pltpu.VMEM(block, BF16)] * 8
        + [
            pltpu.SemaphoreType.DMA((copies,)),
            pltpu.SemaphoreType.DMA((copies,)),
            pltpu.SemaphoreType.DMA((2,)),
        ],
        compiler_params=pltpu.CompilerParams(
            collective_id=0, has_side_effects=True, vmem_limit_bytes=40 * 2**20
        ),
        cost_estimate=pl.CostEstimate(
            flops=6 * 8 * rows * rows * width, bytes_accessed=12 * rows * width,
            transcendentals=3 * 8 * rows * rows,
        ),
    )(images, texts)
    loss, grad_images, grad_texts = pl.pallas_call(
        write_out,
        out_shape=(
            pltpu.HBM((1, rows), F32),
            pltpu.HBM(block, F32),
            pltpu.HBM(block, F32),
        ),
        in_specs=[pl.BlockSpec(memory_space=pltpu.VMEM)] * 3,
        out_specs=(pl.BlockSpec(memory_space=pl.ANY),) * 3,
        scratch_shapes=[pltpu.SemaphoreType.DMA((3,))],
        compiler_params=pltpu.CompilerParams(vmem_limit_bytes=2 * 2**20),
    )(*[pltpu.with_memory_space_constraint(r, pltpu.VMEM) for r in results])
    return loss.reshape(rows), grad_images, grad_texts


def solution(mesh):
    placed = (P("batch", None), P("batch", None))
    return jax.shard_map(
        per_device,
        mesh=mesh,
        in_specs=placed,
        out_specs=(P("batch"), P("batch", None), P("batch", None)),
        check_vma=False,
    )
```

```python
import functools
import math

import jax
import jax.numpy as jnp
from jax import lax
from jax.experimental import pallas as pl
from jax.experimental.pallas import tpu as pltpu
from jax.sharding import PartitionSpec as P

MESH = pl.DeviceIdType.MESH
F32 = jnp.float32
BF16 = jnp.bfloat16
OWN, YP, AP, FAR = 0, 1, 2, 3
CHUNK = 128
HALF = 256
GATHER_LAST = 384
LAST = 320


def pair_terms(products, scale, match):
    logits = products * scale - 1.0
    small = jnp.exp(-jnp.abs(logits))
    inverse = 1.0 / (1.0 + small)
    sig = jnp.where(logits >= 0.0, inverse, small * inverse)
    tail = jnp.where(
        small < 1e-2,
        small * (1.0 - small * (0.5 - small * (1.0 / 3.0))),
        jnp.log(1.0 + small),
    )
    if match is None:
        return (scale * sig).astype(BF16), jnp.maximum(logits, 0.0) + tail
    coef = (scale * (sig - match.astype(F32))).astype(BF16)
    return coef, jnp.maximum(jnp.where(match, -logits, logits), 0.0) + tail


def cuts(last, rows):
    edges = (0, CHUNK, HALF, last, rows)
    return [pl.ds(lo, hi - lo) for lo, hi in zip(edges, edges[1:])]


def kernel(
    images, texts, row_loss, grad_images, grad_texts,
    im, tx, coef, losses, far_losses, grad_b, hold,
    out_y, out_a, out_far, out_b, in_y, in_a, in_far, in_b,
    send, recv, local,
):
    rows, width = images.shape
    scale = 2.0 / math.sqrt(width)
    me = lax.axis_index("batch")
    core = lax.rem(me, 2)
    x = lax.div(me, 32)
    near = me + 32 * (1 - 2 * lax.rem(x, 2))
    other = me + 32 * (3 - 2 * x)
    a = near * (1 - core) + other * core
    b = other * (1 - core) + near * core
    y = me + 16 * (1 - 2 * lax.rem(lax.div(me, 16), 2))

    count = [0]

    def to(src, dst, device):
        k = count[0]
        count[0] += 1
        return pltpu.make_async_remote_copy(
            src, dst, send.at[k], recv.at[k], device_id=(device,), device_id_type=MESH
        )

    chunks = [pl.ds(k * CHUNK, CHUNK) for k in range(rows // CHUNK)]
    image_b = [to(images.at[c], im.at[pl.ds(rows + c.start, CHUNK)], b) for c in chunks]
    text_chunks, back_chunks = cuts(GATHER_LAST, rows), cuts(LAST, rows)
    text_y = [to(texts.at[c], tx.at[YP, c], y) for c in text_chunks]
    text_a = [to(texts.at[c], tx.at[AP, c], a) for c in text_chunks]
    text_far = [to(tx.at[YP, c], tx.at[FAR, c], a) for c in text_chunks[:3]]
    text_far.append(to(tx.at[AP, text_chunks[3]], tx.at[FAR, text_chunks[3]], y))
    back_far = [to(out_far.at[c], in_far.at[c], a) for c in back_chunks[:3]]
    back_far.append(to(out_far.at[back_chunks[3]], in_far.at[back_chunks[3]], y))
    back_y = [to(out_y.at[c], in_y.at[c], y) for c in back_chunks]
    back_a = [to(out_a.at[c], in_a.at[c], a) for c in back_chunks]
    back_b = [to(out_b.at[c], in_b.at[c], b) for c in chunks]
    back_loss = to(losses.at[1], far_losses, b)

    barrier = pltpu.get_barrier_semaphore()
    for device in (a, b, y):
        pl.semaphore_signal(barrier, inc=1, device_id=(device,), device_id_type=MESH)
    pl.semaphore_wait(barrier, 3)

    started = []

    def start(*copies):
        for copy in copies:
            copy.start()
            started.append(copy)

    def arrived(*copies):
        for copy in copies:
            copy.wait_recv()

    start(*image_b, *text_y)
    own_text = pltpu.make_async_copy(texts, tx.at[OWN], local.at[0])
    own_image = pltpu.make_async_copy(images, im.at[pl.ds(0, rows)], local.at[1])
    own_text.start()
    own_image.start()
    own_text.wait()
    own_image.wait()

    def pairs(slot, first, size, side, diagonal=False):
        columns = pl.ds(side * rows, rows)
        products = lax.dot_general(
            tx[slot, first:first + size], im[columns], (((1,), (1,)), ((), ())),
            preferred_element_type=F32,
        )
        match = None
        if diagonal:
            match = lax.broadcasted_iota(jnp.int32, (size, rows), 0) == (
                lax.broadcasted_iota(jnp.int32, (size, rows), 1)
            )
        c, loss = pair_terms(products, scale, match)
        coef[:size, columns] = c
        part = loss.reshape(size // 8, 8, rows).sum(0)
        losses[side] = part if slot == OWN else losses[side] + part

    def text_part(size):
        return jnp.dot(coef[:size], im[...], preferred_element_type=F32)

    def image_part(slot, first, size, side):
        return lax.dot_general(
            coef[:size, side * rows:(side + 1) * rows], tx[slot, first:first + size],
            (((0,), (0,)), ((), ())), preferred_element_type=F32,
        )

    def both_pairs(slot, first):
        pairs(slot, first, HALF, 0)
        pairs(slot, first, HALF, 1)

    def both_images(slot, first):
        grad_images[...] += image_part(slot, first, HALF, 0)
        grad_b[...] += image_part(slot, first, HALF, 1)

    pairs(OWN, 0, rows, 0, True)
    image_b[2].wait_send()
    start(text_a[3])
    image_b[3].wait_send()
    arrived(text_y[0])
    start(text_far[0])
    arrived(*image_b)
    pairs(OWN, 0, rows, 1)
    arrived(text_y[1])
    start(text_far[1])
    grad_texts[...] = text_part(rows)
    grad_images[...] = image_part(OWN, 0, rows, 0)
    arrived(text_a[3])
    start(text_far[3])
    grad_b[...] = image_part(OWN, 0, rows, 1)

    both_pairs(YP, 0)
    hold[:HALF] = text_part(HALF)
    arrived(text_y[2])
    start(text_far[2], text_a[2])
    both_images(YP, 0)

    arrived(text_far[0], text_far[1])
    both_pairs(FAR, 0)
    start(text_a[0])
    out_far[:HALF] = text_part(HALF).astype(BF16)
    start(text_a[1])
    both_images(FAR, 0)

    arrived(text_far[2], text_far[3])
    both_pairs(FAR, HALF)
    out_far[HALF:] = text_part(HALF).astype(BF16)
    start(back_far[3], back_far[0])
    both_images(FAR, HALF)

    arrived(text_a[2])
    both_pairs(AP, HALF)
    part = text_part(HALF)
    out_a[HALF:LAST] = part[:LAST - HALF].astype(BF16)
    hold[LAST:] = part[LAST - HALF:]
    start(back_far[1], back_far[2])
    both_images(AP, HALF)

    arrived(text_y[3])
    both_pairs(YP, HALF)
    part = text_part(HALF)
    hold[HALF:LAST] = part[:LAST - HALF]
    out_y[LAST:] = part[LAST - HALF:].astype(BF16)
    start(back_y[3], back_a[2])
    both_images(YP, HALF)

    def pass_on(k):
        out, back = (out_a, back_a) if k == 3 else (out_y, back_y)
        c = back_chunks[k]
        arrived(back_far[k])
        out[c] = (hold[c] + in_far[c].astype(F32)).astype(BF16)
        start(back[k])

    arrived(text_a[0], text_a[1])
    both_pairs(AP, 0)
    start(back_loss)
    pass_on(0)
    out_a[:HALF] = text_part(HALF).astype(BF16)
    start(back_a[0])
    out_b[...] = (grad_b[...] + image_part(AP, 0, HALF, 1)).astype(BF16)
    start(back_b[0], back_a[1])
    pass_on(1)
    start(back_b[1])
    grad_images[...] += image_part(AP, 0, HALF, 0)
    pass_on(2)
    start(back_b[2])
    pass_on(3)
    start(back_b[3])

    arrived(back_loss)
    row_loss[...] = jnp.sum(losses[0] + far_losses[...], axis=0, keepdims=True) * (1.0 / (8 * rows))
    for k in range(4):
        c = back_chunks[k]
        arrived(back_a[k], back_y[k])
        grad_texts[c] += in_a[c].astype(F32) + in_y[c].astype(F32)
    for k, c in enumerate(chunks):
        arrived(back_b[k])
        grad_images[c] += in_b[c].astype(F32)
    for copy in started:
        if copy is not image_b[2] and copy is not image_b[3]:
            copy.wait_send()


def write_out(*refs):
    sources, targets, done = refs[:3], refs[3:6], refs[6]
    copies = [pltpu.make_async_copy(s, t, done.at[k]) for k, (s, t) in enumerate(zip(sources, targets))]
    for copy in copies:
        copy.start()
    for copy in copies:
        copy.wait()


def per_device(images, texts):
    images = pltpu.with_memory_space_constraint(images, pltpu.HBM)
    texts = pltpu.with_memory_space_constraint(texts, pltpu.HBM)
    rows, width = images.shape
    block = (rows, width)
    copies = 8 * (rows // CHUNK) + 1
    results = pl.pallas_call(
        kernel,
        out_shape=(
            pltpu.VMEM((1, rows), F32),
            pltpu.VMEM(block, F32),
            pltpu.VMEM(block, F32),
        ),
        in_specs=[pl.BlockSpec(memory_space=pl.ANY)] * 2,
        out_specs=(pl.BlockSpec(memory_space=pltpu.VMEM),) * 3,
        scratch_shapes=[
            pltpu.VMEM((2 * rows, width), BF16),
            pltpu.VMEM((4, rows, width), BF16),
            pltpu.VMEM((rows, 2 * rows), BF16),
            pltpu.VMEM((2, 8, rows), F32),
            pltpu.VMEM((8, rows), F32),
            pltpu.VMEM(block, F32),
            pltpu.VMEM(block, F32),
        ]
        + [pltpu.VMEM(block, BF16)] * 8
        + [
            pltpu.SemaphoreType.DMA((copies,)),
            pltpu.SemaphoreType.DMA((copies,)),
            pltpu.SemaphoreType.DMA((2,)),
        ],
        compiler_params=pltpu.CompilerParams(
            collective_id=0, has_side_effects=True, vmem_limit_bytes=40 * 2**20
        ),
        cost_estimate=pl.CostEstimate(
            flops=6 * 8 * rows * rows * width, bytes_accessed=12 * rows * width,
            transcendentals=3 * 8 * rows * rows,
        ),
    )(images, texts)
    loss, grad_images, grad_texts = pl.pallas_call(
        write_out,
        out_shape=(
            pltpu.HBM((1, rows), F32),
            pltpu.HBM(block, F32),
            pltpu.HBM(block, F32),
        ),
        in_specs=[pl.BlockSpec(memory_space=pltpu.VMEM)] * 3,
        out_specs=(pl.BlockSpec(memory_space=pl.ANY),) * 3,
        scratch_shapes=[pltpu.SemaphoreType.DMA((3,))],
        compiler_params=pltpu.CompilerParams(vmem_limit_bytes=2 * 2**20),
    )(*[pltpu.with_memory_space_constraint(r, pltpu.VMEM) for r in results])
    return loss.reshape(rows), grad_images, grad_texts


def solution(mesh):
    placed = (P("batch", None), P("batch", None))
    return jax.shard_map(
        per_device,
        mesh=mesh,
        in_specs=placed,
        out_specs=(P("batch"), P("batch", None), P("batch", None)),
        check_vma=False,
    )
```

```python
import functools
import math

import jax
import jax.numpy as jnp
from jax import lax
from jax.experimental import pallas as pl
from jax.experimental.pallas import tpu as pltpu
from jax.sharding import PartitionSpec as P

MESH = pl.DeviceIdType.MESH
F32 = jnp.float32
BF16 = jnp.bfloat16
OWN, YP, AP, FAR = 0, 1, 2, 3
CHUNK = 128
HALF = 256
FIRST = 224


def pair_terms(products, scale, match):
    logits = products * scale - 1.0
    small = jnp.exp(-jnp.abs(logits))
    inverse = 1.0 / (1.0 + small)
    sig = jnp.where(logits >= 0.0, inverse, small * inverse)
    tail = jnp.where(
        small < 1e-2,
        small * (1.0 - small * (0.5 - small * (1.0 / 3.0))),
        jnp.log(1.0 + small),
    )
    if match is None:
        return (scale * sig).astype(BF16), jnp.maximum(logits, 0.0) + tail
    coef = (scale * (sig - match.astype(F32))).astype(BF16)
    return coef, jnp.maximum(jnp.where(match, -logits, logits), 0.0) + tail


def cuts(*edges):
    return [pl.ds(lo, hi - lo) for lo, hi in zip(edges, edges[1:])]


def kernel(
    images, texts, row_loss, grad_images, grad_texts,
    im, tx, coef, losses, far_losses, grad_b, hold,
    out_y, out_a, out_far, out_b, in_y, in_a, in_far, in_b,
    send, recv, local,
):
    rows, width = images.shape
    scale = 2.0 / math.sqrt(width)
    me = lax.axis_index("batch")
    core = lax.rem(me, 2)
    x = lax.div(me, 32)
    near = me + 32 * (1 - 2 * lax.rem(x, 2))
    other = me + 32 * (3 - 2 * x)
    a = near * (1 - core) + other * core
    b = other * (1 - core) + near * core
    y = me + 16 * (1 - 2 * lax.rem(lax.div(me, 16), 2))

    count = [0]

    def to(src, dst, device):
        k = count[0]
        count[0] += 1
        return pltpu.make_async_remote_copy(
            src, dst, send.at[k], recv.at[k], device_id=(device,), device_id_type=MESH
        )

    chunks = [pl.ds(k * CHUNK, CHUNK) for k in range(rows // CHUNK)]
    image_b = [to(images.at[c], im.at[pl.ds(rows + c.start, CHUNK)], b) for c in chunks]
    text_chunks = cuts(0, CHUNK, HALF, HALF + CHUNK, rows)
    back_chunks = cuts(0, FIRST, HALF, HALF + CHUNK, rows)
    text_y = [to(texts.at[c], tx.at[YP, c], y) for c in text_chunks]
    text_a = [to(texts.at[c], tx.at[AP, c], a) for c in text_chunks]
    text_far = [to(tx.at[YP, c], tx.at[FAR, c], a) for c in text_chunks[:3]]
    text_far.append(to(tx.at[AP, text_chunks[3]], tx.at[FAR, text_chunks[3]], y))
    back_far = [to(out_far.at[back_chunks[0]], in_far.at[back_chunks[0]], y)]
    back_far += [to(out_far.at[c], in_far.at[c], a) for c in back_chunks[1:]]
    back_y = [to(out_y.at[c], in_y.at[c], y) for c in back_chunks]
    back_a = [to(out_a.at[c], in_a.at[c], a) for c in back_chunks]
    back_b = [to(out_b.at[c], in_b.at[c], b) for c in chunks]
    back_loss = to(losses.at[1], far_losses, b)

    own_text = pltpu.make_async_copy(texts, tx.at[OWN], local.at[0])
    own_image = pltpu.make_async_copy(images, im.at[pl.ds(0, rows)], local.at[1])
    own_text.start()
    own_image.start()
    barrier = pltpu.get_barrier_semaphore()
    for device in (a, b, y):
        pl.semaphore_signal(barrier, inc=1, device_id=(device,), device_id_type=MESH)
    pl.semaphore_wait(barrier, 3)

    started = []

    def start(*copies):
        for copy in copies:
            copy.start()
            started.append(copy)

    def arrived(*copies):
        for copy in copies:
            copy.wait_recv()

    start(*image_b, *text_y)
    own_text.wait()
    own_image.wait()

    def own_pairs(first, size):
        columns = slice(first, first + size)
        products = lax.dot_general(
            tx[OWN], im[columns], (((1,), (1,)), ((), ())), preferred_element_type=F32
        )
        match = None
        if first == 0:
            match = lax.broadcasted_iota(jnp.int32, (rows, size), 0) == (
                lax.broadcasted_iota(jnp.int32, (rows, size), 1)
            )
        c, loss = pair_terms(products, scale, match)
        coef[:, columns] = c
        side, at = divmod(first, rows)
        losses[side, :, at:at + size] = loss.reshape(rows // 8, 8, size).sum(0)

    def text_part(size):
        return jnp.dot(coef[:size], im[...], preferred_element_type=F32)

    def image_part(slot, columns, first=0):
        size = rows if slot == OWN else HALF
        return lax.dot_general(
            coef[:size, columns], tx[slot, first:first + size],
            (((0,), (0,)), ((), ())), preferred_element_type=F32,
        )

    def both_pairs(slot, first):
        products = lax.dot_general(
            tx[slot, first:first + HALF], im[...], (((1,), (1,)), ((), ())),
            preferred_element_type=F32,
        )
        c, loss = pair_terms(products, scale, None)
        coef[:HALF] = c
        part = loss.reshape(HALF // 8, 8, 2 * rows).sum(0)
        losses[0] += part[:, :rows]
        losses[1] += part[:, rows:]

    def both_images(slot, first):
        part = image_part(slot, slice(None), first)
        grad_images[...] += part[:rows]
        grad_b[...] += part[rows:]

    def own(first, size):
        columns = slice(first, first + size)
        part = image_part(OWN, columns)
        if first < rows:
            grad_images[...] = part
        else:
            grad_b[first - rows:first - rows + size] = part
        part = jnp.dot(coef[:, columns], im[columns], preferred_element_type=F32)
        grad_texts[...] = part if first == 0 else grad_texts[...] + part

    own_pairs(0, rows)
    own(0, rows)
    arrived(image_b[0], image_b[1])
    own_pairs(rows, HALF)
    image_b[2].wait_send()
    start(text_a[3])
    own(rows, HALF)
    image_b[3].wait_send()
    arrived(text_y[0])
    start(text_far[0])
    arrived(image_b[2], image_b[3])
    own_pairs(rows + HALF, HALF)
    arrived(text_y[1])
    start(text_far[1])
    own(rows + HALF, HALF)
    arrived(text_a[3])
    start(text_far[3])

    both_pairs(YP, 0)
    part = text_part(HALF)
    out_y[:FIRST] = part[:FIRST].astype(BF16)
    hold[FIRST:HALF] = part[FIRST:]
    arrived(text_y[2])
    start(text_far[2], text_a[2])
    both_images(YP, 0)

    arrived(text_far[0], text_far[1])
    both_pairs(FAR, 0)
    start(text_a[0])
    out_far[:HALF] = text_part(HALF).astype(BF16)
    start(text_a[1])
    both_images(FAR, 0)

    arrived(text_far[2], text_far[3])
    start(back_far[0])
    both_pairs(FAR, HALF)
    out_far[HALF:] = text_part(HALF).astype(BF16)
    start(back_far[1], back_far[2])
    both_images(FAR, HALF)

    arrived(text_a[2])
    start(back_y[0])
    both_pairs(AP, HALF)
    start(back_far[3])
    out_a[HALF:] = text_part(HALF).astype(BF16)
    both_images(AP, HALF)

    arrived(text_y[3])
    both_pairs(YP, HALF)
    start(back_a[2])
    hold[HALF:] = text_part(HALF)
    start(back_a[3])
    both_images(YP, HALF)

    def pass_on(k):
        out, back = (out_a, back_a) if k == 0 else (out_y, back_y)
        c = back_chunks[k]
        arrived(back_far[k])
        out[c] = (hold[c] + in_far[c].astype(F32)).astype(BF16)
        start(back[k])

    arrived(text_a[0], text_a[1])
    both_pairs(AP, 0)
    start(back_loss)
    pass_on(1)
    part = text_part(HALF)
    out_a[FIRST:HALF] = part[FIRST:].astype(BF16)
    hold[:FIRST] = part[:FIRST]
    start(back_a[1])
    out_b[...] = (grad_b[...] + image_part(AP, slice(rows, None))).astype(BF16)
    start(back_b[0])
    pass_on(2)
    start(back_b[1])
    grad_images[...] += image_part(AP, slice(0, rows))
    pass_on(3)
    start(back_b[2])
    pass_on(0)
    start(back_b[3])

    arrived(back_loss)
    row_loss[...] = jnp.sum(losses[0] + far_losses[...], axis=0, keepdims=True) * (1.0 / (8 * rows))
    for k in range(4):
        c = back_chunks[k]
        arrived(back_a[k], back_y[k])
        grad_texts[c] += in_a[c].astype(F32) + in_y[c].astype(F32)
    for k, c in enumerate(chunks):
        arrived(back_b[k])
        grad_images[c] += in_b[c].astype(F32)
    for copy in started:
        if copy is not image_b[2] and copy is not image_b[3]:
            copy.wait_send()


def write_out(*refs):
    sources, targets, done = refs[:3], refs[3:6], refs[6]
    rows = sources[1].shape[0]
    copies = [pltpu.make_async_copy(sources[0], targets[0], done.at[0])]
    for k in range(8):
        which, part = 1 + k % 2, pl.ds(k // 2 * (rows // 4), rows // 4)
        copies.append(pltpu.make_async_copy(sources[which].at[part], targets[which].at[part], done.at[1 + k]))
    for copy in copies:
        copy.start()
    for copy in copies:
        copy.wait()


def per_device(images, texts):
    images = pltpu.with_memory_space_constraint(images, pltpu.HBM)
    texts = pltpu.with_memory_space_constraint(texts, pltpu.HBM)
    rows, width = images.shape
    block = (rows, width)
    copies = 8 * (rows // CHUNK) + 1
    results = pl.pallas_call(
        kernel,
        out_shape=(
            pltpu.VMEM((1, rows), F32),
            pltpu.VMEM(block, F32),
            pltpu.VMEM(block, F32),
        ),
        in_specs=[pl.BlockSpec(memory_space=pl.ANY)] * 2,
        out_specs=(pl.BlockSpec(memory_space=pltpu.VMEM),) * 3,
        scratch_shapes=[
            pltpu.VMEM((2 * rows, width), BF16),
            pltpu.VMEM((4, rows, width), BF16),
            pltpu.VMEM((rows, 2 * rows), BF16),
            pltpu.VMEM((2, 8, rows), F32),
            pltpu.VMEM((8, rows), F32),
            pltpu.VMEM(block, F32),
            pltpu.VMEM(block, F32),
        ]
        + [pltpu.VMEM(block, BF16)] * 8
        + [
            pltpu.SemaphoreType.DMA((copies,)),
            pltpu.SemaphoreType.DMA((copies,)),
            pltpu.SemaphoreType.DMA((2,)),
        ],
        compiler_params=pltpu.CompilerParams(
            collective_id=0, has_side_effects=True, vmem_limit_bytes=40 * 2**20
        ),
        cost_estimate=pl.CostEstimate(
            flops=6 * 8 * rows * rows * width, bytes_accessed=12 * rows * width,
            transcendentals=3 * 8 * rows * rows,
        ),
    )(images, texts)
    loss, grad_images, grad_texts = pl.pallas_call(
        write_out,
        out_shape=(
            pltpu.HBM((1, rows), F32),
            pltpu.HBM(block, F32),
            pltpu.HBM(block, F32),
        ),
        in_specs=[pl.BlockSpec(memory_space=pltpu.VMEM)] * 3,
        out_specs=(pl.BlockSpec(memory_space=pl.ANY),) * 3,
        scratch_shapes=[pltpu.SemaphoreType.DMA((9,))],
        compiler_params=pltpu.CompilerParams(vmem_limit_bytes=2 * 2**20),
    )(*[pltpu.with_memory_space_constraint(r, pltpu.VMEM) for r in results])
    return loss.reshape(rows), grad_images, grad_texts


def solution(mesh):
    placed = (P("batch", None), P("batch", None))
    return jax.shard_map(
        per_device,
        mesh=mesh,
        in_specs=placed,
        out_specs=(P("batch"), P("batch", None), P("batch", None)),
        check_vma=False,
    )
```

```python
import functools
import math

import jax
import jax.numpy as jnp
from jax import lax
from jax.experimental import pallas as pl
from jax.experimental.pallas import tpu as pltpu
from jax.sharding import PartitionSpec as P

MESH = pl.DeviceIdType.MESH
F32 = jnp.float32
BF16 = jnp.bfloat16
OWN, YP, AP, FAR = 0, 1, 2, 3
CHUNK = 128
HALF = 256
FIRST = 224


def pair_terms(products, scale, match):
    logits = products * scale - 1.0
    small = jnp.exp(-jnp.abs(logits))
    inverse = 1.0 / (1.0 + small)
    sig = jnp.where(logits >= 0.0, inverse, small * inverse)
    tail = jnp.where(
        small < 1e-2,
        small * (1.0 - small * (0.5 - small * (1.0 / 3.0))),
        jnp.log(1.0 + small),
    )
    if match is None:
        return (scale * sig).astype(BF16), jnp.maximum(logits, 0.0) + tail
    coef = (scale * (sig - match.astype(F32))).astype(BF16)
    return coef, jnp.maximum(jnp.where(match, -logits, logits), 0.0) + tail


def cuts(*edges):
    return [pl.ds(lo, hi - lo) for lo, hi in zip(edges, edges[1:])]


def kernel(
    images, texts, row_loss, grad_images, grad_texts,
    im, tx, coef, losses, far_losses, grad_b, hold,
    out_y, out_a, out_far, out_b, in_y, in_a, in_far, in_b,
    send, recv, local,
):
    rows, width = images.shape
    scale = 2.0 / math.sqrt(width)
    me = lax.axis_index("batch")
    core = lax.rem(me, 2)
    x = lax.div(me, 32)
    near = me + 32 * (1 - 2 * lax.rem(x, 2))
    other = me + 32 * (3 - 2 * x)
    a = near * (1 - core) + other * core
    b = other * (1 - core) + near * core
    y = me + 16 * (1 - 2 * lax.rem(lax.div(me, 16), 2))

    count = [0]

    def to(src, dst, device):
        k = count[0]
        count[0] += 1
        return pltpu.make_async_remote_copy(
            src, dst, send.at[k], recv.at[k], device_id=(device,), device_id_type=MESH
        )

    chunks = [pl.ds(k * CHUNK, CHUNK) for k in range(rows // CHUNK)]
    image_b = [to(images.at[c], im.at[pl.ds(rows + c.start, CHUNK)], b) for c in chunks]
    text_chunks = cuts(0, CHUNK, HALF, HALF + CHUNK, rows)
    back_chunks = cuts(0, FIRST, HALF, HALF + CHUNK, rows)
    text_y = [to(texts.at[c], tx.at[YP, c], y) for c in text_chunks]
    text_a = [to(texts.at[c], tx.at[AP, c], a) for c in text_chunks]
    text_far = [to(tx.at[YP, c], tx.at[FAR, c], a) for c in text_chunks[:3]]
    text_far.append(to(tx.at[AP, text_chunks[3]], tx.at[FAR, text_chunks[3]], y))
    back_far = [to(out_far.at[back_chunks[0]], in_far.at[back_chunks[0]], y)]
    back_far += [to(out_far.at[c], in_far.at[c], a) for c in back_chunks[1:]]
    back_y = [to(out_y.at[c], in_y.at[c], y) for c in back_chunks]
    back_a = [to(out_a.at[c], in_a.at[c], a) for c in back_chunks]
    back_b = [to(out_b.at[c], in_b.at[c], b) for c in chunks]
    back_loss = to(losses.at[1], far_losses, b)

    own_text = pltpu.make_async_copy(texts, tx.at[OWN], local.at[0])
    own_image = pltpu.make_async_copy(images, im.at[pl.ds(0, rows)], local.at[1])
    own_text.start()
    own_image.start()
    barrier = pltpu.get_barrier_semaphore()
    for device in (a, b, y):
        pl.semaphore_signal(barrier, inc=1, device_id=(device,), device_id_type=MESH)
    pl.semaphore_wait(barrier, 3)

    started = []

    def start(*copies):
        for copy in copies:
            copy.start()
            started.append(copy)

    def arrived(*copies):
        for copy in copies:
            copy.wait_recv()

    start(*image_b, *text_y)
    own_text.wait()
    own_image.wait()

    def own_pairs(first, size):
        columns = slice(first, first + size)
        products = lax.dot_general(
            tx[OWN], im[columns], (((1,), (1,)), ((), ())), preferred_element_type=F32
        )
        match = None
        if first == 0:
            match = lax.broadcasted_iota(jnp.int32, (rows, size), 0) == (
                lax.broadcasted_iota(jnp.int32, (rows, size), 1)
            )
        c, loss = pair_terms(products, scale, match)
        coef[:, columns] = c
        side, at = divmod(first, rows)
        losses[side, :, at:at + size] = loss.reshape(rows // 8, 8, size).sum(0)

    def text_part(size):
        return jnp.dot(coef[:size], im[...], preferred_element_type=F32)

    def image_part(slot, columns, first=0):
        size = rows if slot == OWN else HALF
        return lax.dot_general(
            coef[:size, columns], tx[slot, first:first + size],
            (((0,), (0,)), ((), ())), preferred_element_type=F32,
        )

    def both_pairs(slot, first):
        products = lax.dot_general(
            tx[slot, first:first + HALF], im[...], (((1,), (1,)), ((), ())),
            preferred_element_type=F32,
        )
        c, loss = pair_terms(products, scale, None)
        coef[:HALF] = c
        part = loss.reshape(HALF // 8, 8, 2 * rows).sum(0)
        losses[0] += part[:, :rows]
        losses[1] += part[:, rows:]

    def both_images(slot, first):
        part = image_part(slot, slice(None), first)
        grad_images[...] += part[:rows]
        grad_b[...] += part[rows:]

    def own(first, size):
        columns = slice(first, first + size)
        part = image_part(OWN, columns)
        if first < rows:
            grad_images[...] = part
        else:
            grad_b[first - rows:first - rows + size] = part
        part = jnp.dot(coef[:, columns], im[columns], preferred_element_type=F32)
        grad_texts[...] = part if first == 0 else grad_texts[...] + part

    own_pairs(0, rows)
    own(0, rows)
    arrived(image_b[0], image_b[1])
    own_pairs(rows, HALF)
    image_b[2].wait_send()
    arrived(text_y[0])
    start(text_a[3], text_far[0])
    own(rows, HALF)
    image_b[3].wait_send()
    arrived(image_b[2], image_b[3])
    own_pairs(rows + HALF, HALF)
    arrived(text_y[1])
    start(text_far[1])
    own(rows + HALF, HALF)
    arrived(text_a[3])
    start(text_far[3])

    both_pairs(YP, 0)
    part = text_part(HALF)
    out_y[:FIRST] = part[:FIRST].astype(BF16)
    hold[FIRST:HALF] = part[FIRST:]
    arrived(text_y[2])
    start(text_far[2], text_a[2])
    both_images(YP, 0)

    arrived(text_far[0], text_far[1])
    both_pairs(FAR, 0)
    start(text_a[0])
    out_far[:HALF] = text_part(HALF).astype(BF16)
    start(text_a[1])
    both_images(FAR, 0)

    arrived(text_far[2], text_far[3])
    start(back_far[0])
    both_pairs(FAR, HALF)
    out_far[HALF:] = text_part(HALF).astype(BF16)
    start(back_far[1], back_far[2], back_far[3])
    both_images(FAR, HALF)

    arrived(text_a[2])
    start(back_y[0])
    both_pairs(AP, HALF)
    out_a[HALF:] = text_part(HALF).astype(BF16)
    both_images(AP, HALF)

    arrived(text_y[3])
    both_pairs(YP, HALF)
    start(back_a[2])
    hold[HALF:] = text_part(HALF)
    start(back_a[3])
    both_images(YP, HALF)

    def pass_on(k):
        out, back = (out_a, back_a) if k == 0 else (out_y, back_y)
        c = back_chunks[k]
        arrived(back_far[k])
        out[c] = (hold[c] + in_far[c].astype(F32)).astype(BF16)
        start(back[k])

    arrived(text_a[0], text_a[1])
    both_pairs(AP, 0)
    start(back_loss)
    pass_on(1)
    part = text_part(HALF)
    out_a[FIRST:HALF] = part[FIRST:].astype(BF16)
    hold[:FIRST] = part[:FIRST]
    start(back_a[1])
    out_b[...] = (grad_b[...] + image_part(AP, slice(rows, None))).astype(BF16)
    start(back_b[0])
    pass_on(2)
    start(back_b[1])
    pass_on(3)
    start(back_b[2])
    pass_on(0)
    start(back_b[3])
    grad_images[...] += image_part(AP, slice(0, rows))

    arrived(back_loss)
    row_loss[...] = jnp.sum(losses[0] + far_losses[...], axis=0, keepdims=True) * (1.0 / (8 * rows))
    for k in range(4):
        c = back_chunks[k]
        arrived(back_a[k], back_y[k])
        grad_texts[c] += in_a[c].astype(F32) + in_y[c].astype(F32)
    for k, c in enumerate(chunks):
        arrived(back_b[k])
        grad_images[c] += in_b[c].astype(F32)
    for copy in started:
        if copy is not image_b[2] and copy is not image_b[3]:
            copy.wait_send()


def write_out(*refs):
    sources, targets, done = refs[:3], refs[3:6], refs[6]
    rows = sources[1].shape[0]
    copies = [pltpu.make_async_copy(sources[0], targets[0], done.at[0])]
    for k in range(8):
        which, part = 1 + k % 2, pl.ds(k // 2 * (rows // 4), rows // 4)
        copies.append(pltpu.make_async_copy(sources[which].at[part], targets[which].at[part], done.at[1 + k]))
    for copy in copies:
        copy.start()
    for copy in copies:
        copy.wait()


def per_device(images, texts):
    images = pltpu.with_memory_space_constraint(images, pltpu.HBM)
    texts = pltpu.with_memory_space_constraint(texts, pltpu.HBM)
    rows, width = images.shape
    block = (rows, width)
    copies = 8 * (rows // CHUNK) + 1
    results = pl.pallas_call(
        kernel,
        out_shape=(
            pltpu.VMEM((1, rows), F32),
            pltpu.VMEM(block, F32),
            pltpu.VMEM(block, F32),
        ),
        in_specs=[pl.BlockSpec(memory_space=pl.ANY)] * 2,
        out_specs=(pl.BlockSpec(memory_space=pltpu.VMEM),) * 3,
        scratch_shapes=[
            pltpu.VMEM((2 * rows, width), BF16),
            pltpu.VMEM((4, rows, width), BF16),
            pltpu.VMEM((rows, 2 * rows), BF16),
            pltpu.VMEM((2, 8, rows), F32),
            pltpu.VMEM((8, rows), F32),
            pltpu.VMEM(block, F32),
            pltpu.VMEM(block, F32),
        ]
        + [pltpu.VMEM(block, BF16)] * 8
        + [
            pltpu.SemaphoreType.DMA((copies,)),
            pltpu.SemaphoreType.DMA((copies,)),
            pltpu.SemaphoreType.DMA((2,)),
        ],
        compiler_params=pltpu.CompilerParams(
            collective_id=0, has_side_effects=True, vmem_limit_bytes=40 * 2**20
        ),
        cost_estimate=pl.CostEstimate(
            flops=6 * 8 * rows * rows * width, bytes_accessed=12 * rows * width,
            transcendentals=3 * 8 * rows * rows,
        ),
    )(images, texts)
    loss, grad_images, grad_texts = pl.pallas_call(
        write_out,
        out_shape=(
            pltpu.HBM((1, rows), F32),
            pltpu.HBM(block, F32),
            pltpu.HBM(block, F32),
        ),
        in_specs=[pl.BlockSpec(memory_space=pltpu.VMEM)] * 3,
        out_specs=(pl.BlockSpec(memory_space=pl.ANY),) * 3,
        scratch_shapes=[pltpu.SemaphoreType.DMA((9,))],
        compiler_params=pltpu.CompilerParams(vmem_limit_bytes=2 * 2**20),
    )(*[pltpu.with_memory_space_constraint(r, pltpu.VMEM) for r in results])
    return loss.reshape(rows), grad_images, grad_texts


def solution(mesh):
    placed = (P("batch", None), P("batch", None))
    return jax.shard_map(
        per_device,
        mesh=mesh,
        in_specs=placed,
        out_specs=(P("batch"), P("batch", None), P("batch", None)),
        check_vma=False,
    )
```
